32 devices in a mesh: segment: 2 (over y), gx: 2 (over x), gy: 8 (over z, core).
Axes of the slice: x: 2, y: 2, z: 4, core: 2. Of those that a mesh axis runs over, the one named last changes fastest.
Arguments:
- node_latent: bfloat16 [16384, 512], P(('segment', 'gx', 'gy')), may hold values from -6 to 6
- edge_latent: bfloat16 [32768, 512], P(('segment', 'gx', 'gy')), may hold values from -6 to 6
- adjacency: bfloat16 [128, 2, 128, 128], P(('segment', 'gx', 'gy')), may hold values from -0.5 to 0.5
- neighbours: int32 [128, 2], P(('segment', 'gx', 'gy')), may hold values from 0 to 9, as said below
- live: int32 [128, 2], P(('segment', 'gx', 'gy')), may hold values 0 or 1
- send_blocks: int32 [32, 6], P(('segment', 'gx', 'gy')), may hold values from 0 to 3
- w_edge_in: bfloat16 [1536, 512], replicated, may hold values from -0.15625 to 0.15625
- w_edge_out: bfloat16 [512, 512], replicated, may hold values from -0.25 to 0.25
- w_node_in: bfloat16 [1024, 512], replicated, may hold values from -0.1875 to 0.1875
- w_node_out: bfloat16 [512, 512], replicated, may hold values from -0.25 to 0.25
- node_cotangent: bfloat16 [16384, 512], P(('segment', 'gx', 'gy')), may hold values from -6 to 6
- edge_cotangent: bfloat16 [32768, 512], P(('segment', 'gx', 'gy')), may hold values from -6 to 6
Outputs:
- node_out: bfloat16 [16384, 512], P(('segment', 'gx', 'gy'))
- edge_out: bfloat16 [32768, 512], P(('segment', 'gx', 'gy'))
- node_grad: float32 [16384, 512], P(('segment', 'gx', 'gy'))
- grad_edge_in: float32 [786432], P(('segment', 'gx', 'gy'))
- grad_edge_out: float32 [262144], P(('segment', 'gx', 'gy'))
- grad_node_in: float32 [524288], P(('segment', 'gx', 'gy'))
- grad_node_out: float32 [262144], P(('segment', 'gx', 'gy'))
The draws below stay inside these ranges and needn't reach their ends.
Inputs may be any that keep to these rules, and one draw needn't show every extreme that they name: `neighbours`: indices below 4 name the device's own blocks, 4 + j names received block j; on every device each of the six received blocks is named by at least one slot.
All inputs are finite; a program needn't handle non-finite values. No bound on the sum of `live` on one device may be relied on, other than what follows from the above.
Results may differ from the reference program's by a relative error of at most 0.014.
Values may be sent and summed in bfloat16 or wider, within the bound.
A program may use at most 128 MiB of HBM per device.

```python
from functools import partial
import jax
import jax.numpy as jnp
from jax import lax

D = 512
BLK = 128
NB = 4
K = 2
SUBDOMAINS = 32
BLOCKS = 128
NODES = 16384
EDGE_ROWS = 32768
N_SEGMENT = 2
N_GX = 2
N_GY = 8


def draw_neighbours(key, part):
    per_device = BLOCKS // NB
    slot_count = NB * K
    first_key, second_key = jax.random.split(key)
    local_pick = jax.random.randint(first_key, (per_device, slot_count), 0, NB + 6)
    device_keys = jax.random.split(second_key, per_device)

    def shuffle_one(device_key):
        return jax.random.permutation(device_key, slot_count)
    shuffled = jax.vmap(shuffle_one)(device_keys)
    position = jnp.argsort(shuffled, axis=1, stable=True)
    chosen = jnp.where(position < 6, NB + position, local_pick)
    return chosen.reshape(BLOCKS, K).astype(jnp.int32)


def set_ends(drawn, rng, least, top_value):
    shape = drawn.shape
    index_at = [jax.random.randint(jax.random.fold_in(rng, axis), (), 0, shape[axis]) for axis in range(len(shape))]
    drawn = drawn.at[tuple(index_at)].set(least)
    longest = shape.index(max(shape))
    index_at[longest] = (index_at[longest] + 1) % shape[longest]
    return drawn.at[tuple(index_at)].set(top_value)


def steps_of(stream_key, shape, cuts, low, top_value):
    factor_of, own = 1.0, jax.random.fold_in(stream_key, 6)
    for axis_at, blocks in cuts:
        steps = jnp.exp(jax.random.uniform(jax.random.fold_in(own, axis_at), (blocks,), jnp.float32, low / len(cuts), top_value / len(cuts)))
        factor_of = factor_of * jnp.repeat(steps, shape[axis_at] // blocks).reshape([-1 if axis == axis_at else 1 for axis in range(len(shape))])
    return factor_of


def normal_values(key, shape, deviation, most, cuts=(), dtype=jnp.bfloat16):
    values = jax.random.normal(key, shape, jnp.float32) * deviation
    if len(cuts) > 0:
        values = steps_of(key, shape, cuts, -0.22, 0.18) * values
    return jnp.clip(values, min=-most, max=most).astype(dtype)


def setup_inputs(seed: int = 0) -> dict:
    streams_of = jax.random.split(jax.random.key(seed), 13)
    return {
        "node_latent": normal_values(streams_of[0], (NODES, D), 1.0, 6.0, ((0, 32),)),
        "edge_latent": normal_values(streams_of[1], (EDGE_ROWS, D), 1.0, 6.0, ((0, 32),)),
        "adjacency": normal_values(streams_of[2], (BLOCKS, K, BLK, BLK), BLK ** -0.5, 0.5, ((0, 32),)),
        "neighbours": draw_neighbours(jax.random.fold_in(streams_of[12], 71), 0),
        "live": set_ends((jax.random.randint(streams_of[4], (BLOCKS, K), 0, 4) < 3).astype(jnp.int32), jax.random.fold_in(streams_of[4], 1), 0, 1),
        "send_blocks": set_ends(jax.random.randint(streams_of[5], (SUBDOMAINS, 6), 0, NB), jax.random.fold_in(streams_of[5], 1), 0, NB - 1).astype(jnp.int32),
        "w_edge_in": normal_values(streams_of[6], (3 * D, D), (3 * D) ** -0.5, 0.15625),
        "w_edge_out": normal_values(streams_of[7], (D, D), D ** -0.5, 0.25),
        "w_node_in": normal_values(streams_of[8], (2 * D, D), (2 * D) ** -0.5, 0.1875),
        "w_node_out": normal_values(streams_of[9], (D, D), D ** -0.5, 0.25),
        "node_cotangent": normal_values(streams_of[10], (NODES, D), 1.0, 6.0, ((0, 32),)),
        "edge_cotangent": normal_values(streams_of[11], (EDGE_ROWS, D), 1.0, 6.0, ((0, 32),)),
    }


def layer_norm(values):
    average = lax.optimization_barrier(jnp.mean(values, axis=-1, keepdims=True))
    centred = values - average
    return centred * lax.rsqrt(lax.optimization_barrier(jnp.mean(centred * centred, axis=-1, keepdims=True)) + 1e-05)

def edge_part(node_blocks, received, w_edge_in, w_edge_out, edge_rows, adjacency_tiles, picker):
    latent = node_blocks.shape[-1]
    blocks = node_blocks.shape[0]
    block_rows = node_blocks.shape[1]
    degree = picker.shape[0] // blocks
    extended = jnp.concatenate([node_blocks, received], axis=0)
    sources = jnp.einsum('sn,nbd->sbd', picker.astype(jnp.float32), extended.astype(jnp.float32)).astype(jnp.bfloat16)
    mixed_rows = jnp.einsum('sij,sjd->sid', adjacency_tiles.astype(jnp.float32), sources.astype(jnp.float32)).astype(jnp.bfloat16)
    self_term = jnp.dot(node_blocks.reshape(-1, latent), w_edge_in[latent:2 * latent], preferred_element_type=jnp.float32)
    pre_edge = jnp.dot(edge_rows, w_edge_in[:latent], preferred_element_type=jnp.float32) + jnp.dot(mixed_rows.reshape(-1, latent), w_edge_in[2 * latent:], preferred_element_type=jnp.float32)
    pre_edge = (pre_edge.reshape(blocks, degree, block_rows, latent) + self_term.reshape(blocks, 1, block_rows, latent)).reshape(-1, latent)
    edge_hidden = jax.nn.silu(pre_edge).astype(jnp.bfloat16)
    return layer_norm(jnp.dot(edge_hidden, w_edge_out, preferred_element_type=jnp.float32))

def node_part(node_blocks, messages, w_node_in, w_node_out, edge_rows, live_weight):
    latent = node_blocks.shape[-1]
    blocks = node_blocks.shape[0]
    block_rows = node_blocks.shape[1]
    edges_out = (edge_rows.astype(jnp.float32) + messages).astype(jnp.bfloat16)
    gathered = lax.optimization_barrier(jnp.sum(messages.reshape(blocks, -1, block_rows, latent) * live_weight[:, :, None, None], axis=1)).astype(jnp.bfloat16)
    flat_nodes = node_blocks.reshape(-1, latent)
    pre_node = jnp.dot(flat_nodes, w_node_in[:latent], preferred_element_type=jnp.float32) + jnp.dot(gathered.reshape(-1, latent), w_node_in[latent:], preferred_element_type=jnp.float32)
    node_hidden = jax.nn.silu(pre_node).astype(jnp.bfloat16)
    nodes_out = (flat_nodes.astype(jnp.float32) + layer_norm(jnp.dot(node_hidden, w_node_out, preferred_element_type=jnp.float32))).astype(jnp.bfloat16)
    return (nodes_out, edges_out)

def shift_grid(blocks, axis, offset):
    extent = blocks.shape[axis]
    zero_layer = jnp.zeros_like(lax.slice_in_dim(blocks, 0, 1, axis=axis))
    if offset > 0:
        return jnp.concatenate([zero_layer, lax.slice_in_dim(blocks, 0, extent - 1, axis=axis)], axis=axis)
    return jnp.concatenate([lax.slice_in_dim(blocks, 1, extent, axis=axis), zero_layer], axis=axis)

def exchange_grid(faces_grid):
    pieces = [shift_grid(faces_grid[:, :, :, 1], 1, 1), shift_grid(faces_grid[:, :, :, 0], 1, -1), shift_grid(faces_grid[:, :, :, 3], 2, 1), shift_grid(faces_grid[:, :, :, 2], 2, -1), shift_grid(faces_grid[:, :, :, 5], 0, 1), shift_grid(faces_grid[:, :, :, 4], 0, -1)]
    return jnp.stack(pieces, axis=3)

def reference(node_latent, edge_latent, adjacency, neighbours, live, send_blocks, w_edge_in, w_edge_out, w_node_in, w_node_out, node_cotangent, edge_cotangent):
    devices = N_SEGMENT * N_GX * N_GY
    latent = node_latent.shape[1]
    node_grid = node_latent.reshape(N_SEGMENT, N_GX, N_GY, NB, BLK, latent)
    choose = (send_blocks.reshape(N_SEGMENT, N_GX, N_GY, 6)[..., None] == jnp.arange(NB).astype(jnp.int32)).astype(jnp.float32)
    outgoing = jnp.einsum('sxyjn,sxynbd->sxyjbd', choose, node_grid.astype(jnp.float32)).astype(jnp.bfloat16)
    received = exchange_grid(outgoing).reshape(devices, 6, BLK, latent)
    device_items = (node_latent.reshape(devices, NB, BLK, latent), received, edge_latent.reshape(devices, NB * K * BLK, latent), adjacency.reshape(devices, NB * K, BLK, BLK), neighbours.reshape(devices, NB * K), live.reshape(devices, NB, K), node_cotangent.reshape(devices, NB * BLK, latent), edge_cotangent.reshape(devices, NB * K * BLK, latent))

    def visit_device(totals, items):
        node_blocks, recv_blocks, edge_rows, adjacency_tiles, slot_names, live_mask, node_ct, edge_ct = items
        picker = (slot_names[:, None] == jnp.arange(NB + 6).astype(jnp.int32)[None, :]).astype(jnp.bfloat16)
        live_weight = live_mask.astype(jnp.float32)
        messages, edge_pull = jax.vjp(partial(edge_part, edge_rows=edge_rows, adjacency_tiles=adjacency_tiles, picker=picker), node_blocks, recv_blocks, w_edge_in, w_edge_out)
        outputs, node_pull = jax.vjp(partial(node_part, edge_rows=edge_rows, live_weight=live_weight), node_blocks, messages, w_node_in, w_node_out)
        node_direct, message_ct, grad_ni, grad_no = node_pull((node_ct, edge_ct))
        node_indirect, received_ct, grad_ei, grad_eo = edge_pull(message_ct)
        terms = (grad_ei, grad_eo, grad_ni, grad_no)
        totals = tuple((total + term.astype(jnp.float32) for total, term in zip(totals, terms)))
        local_grad = node_direct.astype(jnp.float32) + node_indirect.astype(jnp.float32)
        return (totals, (outputs[0], outputs[1], local_grad, received_ct))
    start = tuple((jnp.zeros(weight.shape, jnp.float32) for weight in (w_edge_in, w_edge_out, w_node_in, w_node_out)))
    totals, stacked = lax.scan(visit_device, start, device_items)
    nodes_out, edges_out, local_grad, received_ct = stacked
    returned = exchange_grid(received_ct.reshape(N_SEGMENT, N_GX, N_GY, 6, BLK, latent))
    node_grad = local_grad.reshape(N_SEGMENT, N_GX, N_GY, NB, BLK, latent) + jnp.einsum('sxyjn,sxyjbd->sxynbd', choose, returned.astype(jnp.float32))
    return (nodes_out.reshape(-1, latent), edges_out.reshape(-1, latent), node_grad.reshape(-1, latent), totals[0].reshape(-1), totals[1].reshape(-1), totals[2].reshape(-1), totals[3].reshape(-1))
```

```python
import functools

import jax
import jax.numpy as jnp
from jax import lax
from jax.experimental import pallas as pl
from jax.experimental.pallas import tpu as pltpu
from jax.sharding import PartitionSpec as P

AXES = ("segment", "gx", "gy")
FACES = ("gx", "gy", "segment")
MESH = pl.DeviceIdType.MESH
F32 = jnp.float32
BF16 = jnp.bfloat16
CORES = 2
TILE = 16


def mm(a, b):
    return lax.dot_general(a, b, (((1,), (0,)), ((), ())), preferred_element_type=F32)


def mm_nt(a, b):
    return lax.dot_general(a, b, (((1,), (1,)), ((), ())), preferred_element_type=F32)


def mm_tn(a, b):
    return lax.dot_general(a, b, (((0,), (0,)), ((), ())), preferred_element_type=F32)


def normalised(values):
    centred = values - jnp.mean(values, axis=-1, keepdims=True)
    scale = lax.rsqrt(jnp.mean(centred * centred, axis=-1, keepdims=True) + 1e-05)
    return centred * scale, scale


def normalised_ct(ct, unit, scale):
    return scale * (
        ct
        - jnp.mean(ct, axis=-1, keepdims=True)
        - unit * jnp.mean(ct * unit, axis=-1, keepdims=True)
    )


def silu_and_slope(v):
    gate = 0.5 * jnp.tanh(0.5 * v) + 0.5
    value = v * gate
    return value, gate + value * (1.0 - gate)


class Halo:
    def __init__(self, source, target, sems, first, sizes):
        self.links = []
        for a, axis in enumerate(FACES):
            here = lax.axis_index(axis)
            for step, out, into in ((1, 2 * a + 1, 2 * a), (-1, 2 * a, 2 * a + 1)):
                other = here + step
                to = (other >= 0) & (other < sizes[axis])
                back = here - step
                frm = (back >= 0) & (back < sizes[axis])
                copy = pltpu.make_async_remote_copy(
                    src_ref=source.at[out],
                    dst_ref=target.at[into],
                    send_sem=sems.at[0, first + into],
                    recv_sem=sems.at[1, first + into],
                    device_id={axis: other},
                    device_id_type=MESH,
                )
                self.links.append((to, frm, copy, into))
        self.target = target

    def start(self):
        for to, frm, copy, into in self.links:
            pl.when(to)(copy.start)

    def zero(self):
        for to, frm, copy, into in self.links:

            @pl.when(jnp.logical_not(frm))
            def _(into=into):
                self.target[into] = jnp.zeros(self.target.shape[1:], self.target.dtype)

    def arrive(self):
        for to, frm, copy, into in self.links:
            pl.when(frm)(copy.wait_recv)

    def sent(self):
        for to, frm, copy, into in self.links:
            pl.when(to)(copy.wait_send)


class Scatter:
    def __init__(self, full, r1, r2, r3, rz, sems, piece, sizes):
        self.full, self.r1, self.r2, self.r3, self.rz = full, r1, r2, r3, rz
        self.depth = sizes["gy"] // CORES
        self.seg, self.gx = lax.axis_index("segment"), lax.axis_index("gx")
        gy = lax.axis_index("gy")
        self.core, self.z = lax.rem(gy, CORES), lax.div(gy, CORES)
        self.sem = lambda side, k: sems.at[side, piece, k]

    def copy(self, src, dst, k, to):
        return pltpu.make_async_remote_copy(
            src_ref=src,
            dst_ref=dst,
            send_sem=self.sem(0, k),
            recv_sem=self.sem(1, k),
            device_id=to,
            device_id_type=MESH,
        )

    def core_copy(self):
        other = 1 - self.core
        return self.copy(
            self.full.at[:, :, :, other], self.r1, 0, {"gy": self.z * CORES + other}
        )

    def first_copy(self, core):
        if core == 0:
            return self.copy(self.r1.at[:, 1 - self.gx], self.r2, 1, {"gx": 1 - self.gx})
        return self.copy(self.r1.at[1 - self.seg], self.r2, 1, {"segment": 1 - self.seg})

    def second_copy(self, core):
        if core == 0:
            return self.copy(self.r2.at[1 - self.seg], self.r3, 2, {"segment": 1 - self.seg})
        return self.copy(self.r2.at[1 - self.gx], self.r3, 2, {"gx": 1 - self.gx})

    def last_copy(self, step):
        to = lax.rem(self.z + step, self.depth)
        return self.copy(
            self.r3.at[to], self.rz.at[step - 1], 2 + step, {"gy": to * CORES + self.core}
        )

    def by_core(self, act):
        for core in range(CORES):
            pl.when(self.core == core)(functools.partial(act, core))

    def start(self):
        self.core_copy().start()

    def step1(self):
        self.core_copy().wait_recv()
        for s in range(2):
            for x in range(2):

                def body(z, _):
                    self.r1[s, x, z] = self.r1[s, x, z] + self.full[s, x, z, self.core]
                    return 0

                lax.fori_loop(0, self.depth, body, 0)
        self.by_core(lambda core: self.first_copy(core).start())

    def step2(self):
        def act(core):
            self.first_copy(core).wait_recv()

            def body(z, _):
                for h in range(2):
                    mine = self.r1[h, self.gx, z] if core == 0 else self.r1[self.seg, h, z]
                    self.r2[h, z] = self.r2[h, z] + mine
                return 0

            lax.fori_loop(0, self.depth, body, 0)
            self.second_copy(core).start()

        self.by_core(act)

    def step3(self):
        def act(core):
            self.second_copy(core).wait_recv()
            mine = self.seg if core == 0 else self.gx

            def body(z, _):
                self.r3[z] = self.r3[z] + self.r2[mine, z]
                return 0

            lax.fori_loop(0, self.depth, body, 0)

        self.by_core(act)
        for step in range(1, self.depth):
            self.last_copy(step).start()

    def step4(self):
        total = self.r3[self.z].astype(F32)
        for step in range(1, self.depth):
            self.last_copy(step).wait_recv()
            total = total + self.rz[step - 1].astype(F32)
        return total

    def sent(self):
        self.core_copy().wait_send()
        self.by_core(lambda core: self.first_copy(core).wait_send())
        self.by_core(lambda core: self.second_copy(core).wait_send())
        for step in range(1, self.depth):
            self.last_copy(step).wait_send()


def layer_kernel(sizes, pieces, scatter, *refs):
    (node, edge, adj, nb, live, sb, wei, weo, wni, wno, nct, ect) = refs[:12]
    node_out, edge_out, node_grad = refs[12:15]
    grads = refs[15:19]
    (out, ext, rct, ret, pre, spread, mixed, hid, slope, unit, scale, gath, hidn, dpren, dyn, dgath,
     dmix, dsum, halo_sems) = refs[19:38]
    rest = refs[38:]
    blocks, block, latent = node.shape
    degree = adj.shape[0] // blocks
    span = degree * block
    rows = blocks * block

    seg, gx, gy = (lax.axis_index(a) for a in AXES)
    barrier = pltpu.get_barrier_semaphore()
    count = 0
    greet = []
    for axis in FACES:
        here = lax.axis_index(axis)
        for step in (1, -1):
            other = here + step
            there = (other >= 0) & (other < sizes[axis])
            greet.append((there, {axis: other}))
            count = count + there.astype(jnp.int32)
    for there, to in greet:

        @pl.when(there)
        def _(to=to):
            pl.semaphore_signal(barrier, inc=1, device_id=to, device_id_type=MESH)

    if scatter:
        core, z, depth = lax.rem(gy, CORES), lax.div(gy, CORES), sizes["gy"] // CORES
        for step in range(1, depth):
            to = {"gy": lax.rem(z + step, depth) * CORES + core}
            pl.semaphore_signal(barrier, inc=1, device_id=to, device_id_type=MESH)
        count = count + (depth - 1)
    pl.semaphore_wait(barrier, count)

    for j in range(6):
        out[j] = node[sb[0, j]]
    ahead = Halo(out, ext.at[pl.ds(blocks, 6)], halo_sems, 0, sizes)
    ahead.start()
    ahead.zero()

    if scatter:
        per = len(rest) // 2
        del per
        fulls, bufs, sems = rest[0:3], rest[3:15], rest[15]
        moves = [
            Scatter(fulls[i], *bufs[4 * i : 4 * i + 4], sems, i, sizes) for i in range(3)
        ]

    def put(piece, row, value, part=0):
        if not scatter:
            grads[piece][row : row + value.shape[0], :] = value.astype(BF16)
            return
        index, base = pieces[piece]
        own = grads[piece].shape[0]
        value = value.astype(BF16)
        depth = sizes["gy"] // CORES
        for t in range(0, value.shape[0], TILE):
            d, at = divmod(row + t, own)
            d, c = divmod(d, CORES)
            d, z = divmod(d, depth)
            s, x = divmod(d, sizes["gx"])
            fulls[index][s, x, z, c, base + at : base + at + TILE, :] = value[t : t + TILE]

    def weight_grad(piece, row, left, right):
        half = latent // 2
        for h in range(2):
            put(piece, row + h * half, mm_tn(left[:, h * half : (h + 1) * half], right[...]))

    for n in range(blocks):
        ext[n] = node[n]

    def first(n, _):
        at = pl.multiple_of(n * span, span)
        own = mm(node[n], wei[latent : 2 * latent, :])
        whole = mm(edge[pl.ds(at, span), :], wei[:latent, :])
        for k in range(degree):
            pre[pl.ds(pl.multiple_of(at + k * block, block), block), :] = (
                whole[k * block : (k + 1) * block] + own
            )
        return 0

    lax.fori_loop(0, blocks, first, 0)

    def picked(n, _):
        at = pl.multiple_of(n * span, span)
        for k in range(degree):
            turned = adj[n * degree + k].T
            for j in range(blocks + 6):
                pick = jnp.where(nb[n, k] == j, 1.0, 0.0).astype(F32)
                spread[j * block : (j + 1) * block, pl.ds(pl.multiple_of(at + k * block, block), block)] = (
                    turned.astype(F32) * pick
                ).astype(BF16)
        return 0

    lax.fori_loop(0, blocks, picked, 0)

    ahead.arrive()

    def forward(n, _):
        at = pl.multiple_of(n * span, span)
        here = pl.ds(at, span)
        mix = jnp.concatenate(
            [mm(adj[n * degree + k], ext[nb[n, k]]) for k in range(degree)], axis=0
        ).astype(BF16)
        mixed[here, :] = mix
        value, bend = silu_and_slope(pre[here, :] + mm(mix, wei[2 * latent :, :]))
        value = value.astype(BF16)
        hid[here, :] = value
        slope[here, :] = bend
        message, spreadness = normalised(mm(value, weo[...]))
        unit[here, :] = message
        scale[here, :] = jnp.broadcast_to(spreadness, (span, scale.shape[1]))
        edge_out[here, :] = (edge[here, :].astype(F32) + message).astype(BF16)
        total = message[:block] * live[n, 0].astype(F32)
        for k in range(1, degree):
            total = total + message[k * block : (k + 1) * block] * live[n, k].astype(F32)
        gath[pl.ds(pl.multiple_of(n * block, block), block), :] = total.astype(BF16)
        return 0

    lax.fori_loop(0, blocks, forward, 0)

    group = 2 if blocks % 2 == 0 else 1
    tall = group * block

    def nodes(g, _):
        at = pl.multiple_of(g * tall, tall)
        here = pl.ds(at, tall)
        latents = jnp.concatenate([node[g * group + i] for i in range(group)], axis=0)
        value, bend = silu_and_slope(
            mm(latents, wni[:latent, :]) + mm(gath[here, :], wni[latent:, :])
        )
        value = value.astype(BF16)
        hidn[here, :] = value
        update, spreadness = normalised(mm(value, wno[...]))
        node_out[here, :] = (latents.astype(F32) + update).astype(BF16)
        ct = nct[here, :].astype(F32)
        dy = normalised_ct(ct, update, spreadness).astype(BF16)
        dyn[here, :] = dy
        dp = (mm_nt(dy, wno[...]) * bend).astype(BF16)
        dpren[here, :] = dp
        node_grad[here, :] = ct + mm_nt(dp, wni[:latent, :])
        dgath[here, :] = mm_nt(dp, wni[latent:, :])
        return 0

    lax.fori_loop(0, blocks // group, nodes, 0)

    flat = ext.at[pl.ds(0, blocks)][...].reshape(rows, latent)
    weight_grad(2, 0, flat, dpren)
    weight_grad(2, latent, gath, dpren)
    weight_grad(3, 0, hidn, dyn)
    if scatter:
        moves[0].start()

    def backward(n, _):
        at = pl.multiple_of(n * span, span)
        here = pl.ds(at, span)
        back = dgath[pl.ds(pl.multiple_of(n * block, block), block), :]
        ct = ect[here, :].astype(F32) + jnp.concatenate(
            [back * live[n, k].astype(F32) for k in range(degree)], axis=0
        )
        dy = normalised_ct(ct, unit[here, :], scale[here, :1]).astype(BF16)
        unit[here, :] = dy.astype(F32)
        dp = mm_nt(dy, weo[...]) * slope[here, :]
        total = dp[:block]
        for k in range(1, degree):
            total = total + dp[k * block : (k + 1) * block]
        dsum[pl.ds(pl.multiple_of(n * block, block), block), :] = total.astype(BF16)
        dp = dp.astype(BF16)
        pre[here, :] = dp.astype(F32)
        dmix[here, :] = mm_nt(dp, wei[2 * latent :, :]).astype(BF16)
        return 0

    half = blocks // 2
    lax.fori_loop(0, half, backward, 0)
    if scatter:
        moves[0].step1()
    lax.fori_loop(half, blocks, backward, 0)

    for j in range(6):
        at = (blocks + j) * block
        rct[j] = mm(spread[at : at + block, :], dmix[...]).astype(BF16)
    behind = Halo(rct, ret, halo_sems, 6, sizes)
    behind.start()
    behind.zero()

    weight_grad(1, 0, hid, unit[...].astype(BF16))
    if scatter:
        moves[1].start()
    dp = pre[...].astype(BF16)
    weight_grad(0, 0, edge, dp)
    if scatter:
        moves[0].step2()
        moves[1].step1()
    weight_grad(0, latent, flat, dsum)
    weight_grad(0, 2 * latent, mixed, dp)
    if scatter:
        moves[2].start()

    node_grad[...] += mm(spread[: blocks * block, :], dmix[...]) + mm_nt(
        dsum[...], wei[latent : 2 * latent, :]
    )
    if scatter:
        moves[2].step1()
        moves[0].step3()
        moves[1].step2()

    behind.arrive()
    for n in range(blocks):
        total = node_grad[n * block : (n + 1) * block, :]
        for j in range(6):
            pick = jnp.where(sb[0, j] == n, 1.0, 0.0).astype(F32)
            total = total + ret[j].astype(F32) * pick
        node_grad[n * block : (n + 1) * block, :] = total

    if scatter:
        moves[1].step3()
        moves[2].step2()
        nodes_total = moves[0].step4()
        own = grads[2].shape[0]
        grads[2][...] = nodes_total[:own]
        grads[3][...] = nodes_total[own:]
        grads[1][...] = moves[1].step4()
        moves[2].step3()
        grads[0][...] = moves[2].step4()
        for move in moves:
            move.sent()
    ahead.sent()
    behind.sent()


def layer(sizes, *args):
    (node, edge, adj, nb, live, sb, wei, weo, wni, wno, nct, ect) = args
    rows, latent = node.shape
    blocks, degree = nb.shape
    block = adj.shape[-1]
    edges = edge.shape[0]
    devices = sizes["segment"] * sizes["gx"] * sizes["gy"]
    weights = (wei, weo, wni, wno)
    scatter = (
        sizes["segment"] == 2
        and sizes["gx"] == 2
        and sizes["gy"] % CORES == 0
        and all(w.shape[0] % (devices * TILE) == 0 for w in weights)
    )
    shapes = [
        jax.ShapeDtypeStruct((rows, latent), BF16),
        jax.ShapeDtypeStruct((edges, latent), BF16),
        jax.ShapeDtypeStruct((rows, latent), F32),
    ]
    scratch = [
        pltpu.VMEM((6, block, latent), BF16),
        pltpu.VMEM((blocks + 6, block, latent), BF16),
        pltpu.VMEM((6, block, latent), BF16),
        pltpu.VMEM((6, block, latent), BF16),
        pltpu.VMEM((edges, latent), F32),
        pltpu.VMEM(((blocks + 6) * block, edges), BF16),
        pltpu.VMEM((edges, latent), BF16),
        pltpu.VMEM((edges, latent), BF16),
        pltpu.VMEM((edges, latent), F32),
        pltpu.VMEM((edges, latent), F32),
        pltpu.VMEM((edges, 128), F32),
        pltpu.VMEM((rows, latent), BF16),
        pltpu.VMEM((rows, latent), BF16),
        pltpu.VMEM((rows, latent), BF16),
        pltpu.VMEM((rows, latent), BF16),
        pltpu.VMEM((rows, latent), F32),
        pltpu.VMEM((edges, latent), BF16),
        pltpu.VMEM((rows, latent), BF16),
        pltpu.SemaphoreType.DMA((2, 12)),
    ]
    pieces = None
    if scatter:
        own = [w.shape[0] // devices for w in weights]
        shapes += [jax.ShapeDtypeStruct((r, latent), F32) for r in own]
        pieces = {2: (0, 0), 3: (0, own[2]), 1: (1, 0), 0: (2, 0)}
        s, x, z = sizes["segment"], sizes["gx"], sizes["gy"] // CORES
        heights = (own[2] + own[3], own[1], own[0])
        scratch += [pltpu.VMEM((s, x, z, CORES, r, latent), BF16) for r in heights]
        for r in heights:
            scratch += [
                pltpu.VMEM((s, x, z, r, latent), BF16),
                pltpu.VMEM((2, z, r, latent), BF16),
                pltpu.VMEM((z, r, latent), BF16),
                pltpu.VMEM((z - 1, r, latent), BF16),
            ]
        scratch.append(pltpu.SemaphoreType.DMA((2, 3, 2 + z)))
    else:
        shapes += [jax.ShapeDtypeStruct(w.shape, BF16) for w in weights]
    vmem = pl.BlockSpec(memory_space=pltpu.VMEM)
    smem = pl.BlockSpec(memory_space=pltpu.SMEM)
    results = pl.pallas_call(
        functools.partial(layer_kernel, sizes, pieces, scatter),
        out_shape=shapes,
        in_specs=[vmem, vmem, vmem, smem, smem, smem] + [vmem] * 6,
        out_specs=[vmem] * 7,
        scratch_shapes=scratch,
        compiler_params=pltpu.CompilerParams(
            collective_id=0, has_side_effects=True, vmem_limit_bytes=60 * 1024 * 1024
        ),
    )(
        node.reshape(blocks, block, latent),
        edge,
        adj.reshape(blocks * degree, block, block),
        nb,
        live,
        sb,
        wei,
        weo,
        wni,
        wno,
        nct,
        ect,
    )
    shares = results[3:]
    if scatter:
        shares = [g.reshape(-1) for g in shares]
    else:
        shares = [
            lax.psum_scatter(g.astype(F32).reshape(-1), AXES, scatter_dimension=0, tiled=True)
            for g in shares
        ]
    return tuple(results[:3]) + tuple(shares)


def solution(mesh):
    split, copied = P(AXES, None), P()
    return jax.shard_map(
        functools.partial(layer, dict(mesh.shape)),
        mesh=mesh,
        in_specs=(split, split, P(AXES, None, None, None), split, split, split)
        + (copied,) * 4
        + (split, split),
        out_specs=(split, split, split) + (P(AXES),) * 4,
        check_vma=False,
    )
```

```python
import functools

import jax
import jax.numpy as jnp
from jax import lax
from jax.experimental import pallas as pl
from jax.experimental.pallas import tpu as pltpu
from jax.sharding import PartitionSpec as P

AXES = ("segment", "gx", "gy")
FACES = ("gx", "gy", "segment")
MESH = pl.DeviceIdType.MESH
F32 = jnp.float32
BF16 = jnp.bfloat16
CORES = 2
TILE = 16


def mm(a, b):
    return lax.dot_general(a, b, (((1,), (0,)), ((), ())), preferred_element_type=F32)


def mm_nt(a, b):
    return lax.dot_general(a, b, (((1,), (1,)), ((), ())), preferred_element_type=F32)


def mm_tn(a, b):
    return lax.dot_general(a, b, (((0,), (0,)), ((), ())), preferred_element_type=F32)


def normalised(values):
    centred = values - jnp.mean(values, axis=-1, keepdims=True)
    scale = lax.rsqrt(jnp.mean(centred * centred, axis=-1, keepdims=True) + 1e-05)
    return centred * scale, scale


def normalised_ct(ct, unit, scale):
    return scale * (
        ct
        - jnp.mean(ct, axis=-1, keepdims=True)
        - unit * jnp.mean(ct * unit, axis=-1, keepdims=True)
    )


def silu_and_slope(v):
    gate = 0.5 * jnp.tanh(0.5 * v) + 0.5
    value = v * gate
    return value, gate + value * (1.0 - gate)


class Halo:
    def __init__(self, source, target, sems, first, sizes):
        self.links = []
        for a, axis in enumerate(FACES):
            here = lax.axis_index(axis)
            for step, out, into in ((1, 2 * a + 1, 2 * a), (-1, 2 * a, 2 * a + 1)):
                other = here + step
                to = (other >= 0) & (other < sizes[axis])
                back = here - step
                frm = (back >= 0) & (back < sizes[axis])
                copy = pltpu.make_async_remote_copy(
                    src_ref=source.at[out],
                    dst_ref=target.at[into],
                    send_sem=sems.at[0, first + into],
                    recv_sem=sems.at[1, first + into],
                    device_id={axis: other},
                    device_id_type=MESH,
                )
                self.links.append((to, frm, copy, into))
        self.target = target

    def start(self):
        for to, frm, copy, into in self.links:
            pl.when(to)(copy.start)

    def zero(self):
        for to, frm, copy, into in self.links:

            @pl.when(jnp.logical_not(frm))
            def _(into=into):
                self.target[into] = jnp.zeros(self.target.shape[1:], self.target.dtype)

    def arrive(self):
        for to, frm, copy, into in self.links:
            pl.when(frm)(copy.wait_recv)

    def sent(self):
        for to, frm, copy, into in self.links:
            pl.when(to)(copy.wait_send)


class Scatter:
    def __init__(self, full, r1, r2, r3, rz, sems, piece, sizes):
        self.full, self.r1, self.r2, self.r3, self.rz = full, r1, r2, r3, rz
        self.depth = sizes["gy"] // CORES
        self.seg, self.gx = lax.axis_index("segment"), lax.axis_index("gx")
        gy = lax.axis_index("gy")
        self.core, self.z = lax.rem(gy, CORES), lax.div(gy, CORES)
        self.sem = lambda side, k: sems.at[side, piece, k]

    def copy(self, src, dst, k, to):
        return pltpu.make_async_remote_copy(
            src_ref=src,
            dst_ref=dst,
            send_sem=self.sem(0, k),
            recv_sem=self.sem(1, k),
            device_id=to,
            device_id_type=MESH,
        )

    def core_copy(self):
        other = 1 - self.core
        return self.copy(
            self.full.at[:, :, :, other], self.r1, 0, {"gy": self.z * CORES + other}
        )

    def first_copy(self, core):
        if core == 0:
            return self.copy(self.r1.at[:, 1 - self.gx], self.r2, 1, {"gx": 1 - self.gx})
        return self.copy(self.r1.at[1 - self.seg], self.r2, 1, {"segment": 1 - self.seg})

    def second_copy(self, core):
        if core == 0:
            return self.copy(self.r2.at[1 - self.seg], self.r3, 2, {"segment": 1 - self.seg})
        return self.copy(self.r2.at[1 - self.gx], self.r3, 2, {"gx": 1 - self.gx})

    def last_copy(self, step):
        to = lax.rem(self.z + step, self.depth)
        return self.copy(
            self.r3.at[to], self.rz.at[step - 1], 2 + step, {"gy": to * CORES + self.core}
        )

    def by_core(self, act):
        for core in range(CORES):
            pl.when(self.core == core)(functools.partial(act, core))

    def start(self):
        self.core_copy().start()

    def step1(self):
        self.core_copy().wait_recv()
        for s in range(2):
            for x in range(2):
                for z in range(self.depth):
                    self.r1[s, x, z] = self.r1[s, x, z] + self.full[s, x, z, self.core]
        self.by_core(lambda core: self.first_copy(core).start())

    def step2(self):
        def act(core):
            self.first_copy(core).wait_recv()

            for z in range(self.depth):
                for h in range(2):
                    mine = self.r1[h, self.gx, z] if core == 0 else self.r1[self.seg, h, z]
                    self.r2[h, z] = self.r2[h, z] + mine
            self.second_copy(core).start()

        self.by_core(act)

    def step3(self):
        def act(core):
            self.second_copy(core).wait_recv()
            mine = self.seg if core == 0 else self.gx

            for z in range(self.depth):
                self.r3[z] = self.r3[z] + self.r2[mine, z]

        self.by_core(act)
        for step in range(1, self.depth):
            self.last_copy(step).start()

    def step4(self):
        total = self.r3[self.z].astype(F32)
        for step in range(1, self.depth):
            self.last_copy(step).wait_recv()
            total = total + self.rz[step - 1].astype(F32)
        return total

    def sent(self):
        self.core_copy().wait_send()
        self.by_core(lambda core: self.first_copy(core).wait_send())
        self.by_core(lambda core: self.second_copy(core).wait_send())
        for step in range(1, self.depth):
            self.last_copy(step).wait_send()


def layer_kernel(sizes, plan, scatter, *refs):
    nb, live, sb = refs[:3]
    operands = refs[3:12]
    node_out_hbm, edge_out_hbm, node_grad = refs[12:15]
    grads = refs[15:19]
    held = refs[19:28]
    (node, edge, wei, adj, weo, wni, wno, nct, ect) = held
    (node_out, edge_out, out, ext, rct, ret, pre, spread, mixed, hid, slope, unit, scale, gath, hidn,
     dpren, dyn, dgath, dmix, dsum, dye, dpe, load_sems, halo_sems) = refs[28:52]
    rest = refs[52:]
    blocks, block, latent = node.shape
    degree = adj.shape[0] // blocks
    span = degree * block
    rows = blocks * block

    loads = {}
    for i, (src, dst) in enumerate(zip(operands, held)):
        loads[i] = pltpu.make_async_copy(src, dst, load_sems.at[i])
        loads[i].start()

    gy = lax.axis_index("gy")
    barrier = pltpu.get_barrier_semaphore()
    count = 0
    greet = []
    for axis in FACES:
        here = lax.axis_index(axis)
        for step in (1, -1):
            other = here + step
            there = (other >= 0) & (other < sizes[axis])
            greet.append((there, {axis: other}))
            count = count + there.astype(jnp.int32)
    for there, to in greet:

        @pl.when(there)
        def _(to=to):
            pl.semaphore_signal(barrier, inc=1, device_id=to, device_id_type=MESH)

    if scatter:
        core, z, depth = lax.rem(gy, CORES), lax.div(gy, CORES), sizes["gy"] // CORES
        for step in range(1, depth):
            to = {"gy": lax.rem(z + step, depth) * CORES + core}
            pl.semaphore_signal(barrier, inc=1, device_id=to, device_id_type=MESH)
        count = count + (depth - 1)
    loads[0].wait()
    for j in range(6):
        out[j] = node[sb[0, j]]
    pl.semaphore_wait(barrier, count)

    ahead = Halo(out, ext.at[pl.ds(blocks, 6)], halo_sems, 0, sizes)
    ahead.start()
    ahead.zero()

    moves = []
    if scatter:
        pieces, starts, total = plan
        fulls, bufs, sems = rest[:total], rest[total : 5 * total], rest[5 * total]
        moves = [
            Scatter(fulls[i], *bufs[4 * i : 4 * i + 4], sems, i, sizes) for i in range(total)
        ]

    def put(weight, row, value):
        value = value.astype(BF16)
        if not scatter:
            grads[weight][row : row + value.shape[0], :] = value
            return
        own = starts[weight]
        depth = sizes["gy"] // CORES
        for t in range(0, value.shape[0], TILE):
            d, at = divmod(row + t, own)
            d, c = divmod(d, CORES)
            d, z = divmod(d, depth)
            s, x = divmod(d, sizes["gx"])
            index, base = pieces[weight, at // TILE]
            fulls[index][s, x, z, c, base : base + TILE, :] = value[t : t + TILE]

    def give_piece(index, value):
        for (weight, sub), (piece, base) in pieces.items():
            if piece == index:
                ratio = latent // 128
                for q in range(ratio):
                    part = value[base : base + TILE, q * 128 : (q + 1) * 128]
                    at = sub * TILE * ratio + q
                    grads[weight][pl.ds(at, TILE, stride=ratio), :] = part

    group = 2 if blocks % 2 == 0 else 1
    tall = group * block
    wide = group * span

    loads[1].wait()
    loads[2].wait()
    for n in range(blocks):
        ext[n] = node[n]

    def first(g, _):
        at = pl.multiple_of(g * wide, wide)
        latents = jnp.concatenate([node[g * group + i] for i in range(group)], axis=0)
        own = mm(latents, wei[latent : 2 * latent, :])
        whole = mm(edge[pl.ds(at, wide), :], wei[:latent, :])
        for i in range(group):
            for k in range(degree):
                off = i * span + k * block
                pre[pl.ds(pl.multiple_of(at + off, block), block), :] = (
                    whole[off : off + block] + own[i * block : (i + 1) * block]
                )
        return 0

    lax.fori_loop(0, blocks // group, first, 0)
    loads[3].wait()

    def picked(n, _):
        for k in range(degree):
            turned = adj[n * degree + k].T.astype(F32)
            col = pl.ds(pl.multiple_of(n * span + k * block, block), block)
            for j in range(blocks + 6):
                pick = jnp.where(nb[k, n] == j, 1.0, 0.0).astype(F32)
                spread[j * block : (j + 1) * block, col] = (turned * pick).astype(BF16)
        return 0

    lax.fori_loop(0, blocks, picked, 0)
    loads[4].wait()
    ahead.arrive()

    def forward(g, _):
        at = pl.multiple_of(g * wide, wide)
        here = pl.ds(at, wide)
        for i in range(group):
            n = g * group + i
            for k in range(degree):
                off = pl.multiple_of(at + i * span + k * block, block)
                mixed[pl.ds(off, block), :] = mm(adj[n * degree + k], ext[nb[k, n]]).astype(BF16)
        value, bend = silu_and_slope(pre[here, :] + mm(mixed[here, :], wei[2 * latent :, :]))
        value = value.astype(BF16)
        hid[here, :] = value
        slope[here, :] = bend
        message, spreadness = normalised(mm(value, weo[...]))
        unit[here, :] = message
        scale[here, :] = jnp.broadcast_to(spreadness, (wide, scale.shape[1]))
        edge_out[here, :] = (edge[here, :].astype(F32) + message).astype(BF16)
        for i in range(group):
            n = g * group + i
            off = i * span
            total = message[off : off + block] * live[0, n].astype(F32)
            for k in range(1, degree):
                part = message[off + k * block : off + (k + 1) * block]
                total = total + part * live[k, n].astype(F32)
            gath[pl.ds(pl.multiple_of(n * block, block), block), :] = total.astype(BF16)
        return 0

    lax.fori_loop(0, blocks // group, forward, 0)
    edge_done = pltpu.make_async_copy(edge_out, edge_out_hbm, load_sems.at[9])
    edge_done.start()
    for i in (5, 6, 7):
        loads[i].wait()

    def nodes(g, _):
        at = pl.multiple_of(g * tall, tall)
        here = pl.ds(at, tall)
        latents = jnp.concatenate([node[g * group + i] for i in range(group)], axis=0)
        value, bend = silu_and_slope(
            mm(latents, wni[:latent, :]) + mm(gath[here, :], wni[latent:, :])
        )
        value = value.astype(BF16)
        hidn[here, :] = value
        update, spreadness = normalised(mm(value, wno[...]))
        node_out[here, :] = (latents.astype(F32) + update).astype(BF16)
        ct = nct[here, :].astype(F32)
        dy = normalised_ct(ct, update, spreadness).astype(BF16)
        dyn[here, :] = dy
        dp = (mm_nt(dy, wno[...]) * bend).astype(BF16)
        dpren[here, :] = dp
        node_grad[here, :] = ct + mm_nt(dp, wni[:latent, :])
        dgath[here, :] = mm_nt(dp, wni[latent:, :])
        return 0

    lax.fori_loop(0, blocks // group, nodes, 0)
    node_done = pltpu.make_async_copy(node_out, node_out_hbm, load_sems.at[10])
    node_done.start()

    flat = ext.at[pl.ds(0, blocks)][...].reshape(rows, latent)
    put(2, 0, mm_tn(flat, dpren[...]))
    put(2, latent, mm_tn(gath[...], dpren[...]))
    put(3, 0, mm_tn(hidn[...], dyn[...]))
    if scatter:
        moves[0].start()
    loads[8].wait()

    def backward(g, _):
        at = pl.multiple_of(g * wide, wide)
        here = pl.ds(at, wide)
        back = dgath[pl.ds(pl.multiple_of(g * tall, tall), tall), :]
        ct = ect[here, :].astype(F32) + jnp.concatenate(
            [
                back[i * block : (i + 1) * block] * live[k, g * group + i].astype(F32)
                for i in range(group)
                for k in range(degree)
            ],
            axis=0,
        )
        dy = normalised_ct(ct, unit[here, :], scale[here, :1]).astype(BF16)
        dye[here, :] = dy
        dp = mm_nt(dy, weo[...]) * slope[here, :]
        for i in range(group):
            off = i * span
            total = dp[off : off + block]
            for k in range(1, degree):
                total = total + dp[off + k * block : off + (k + 1) * block]
            dsum[pl.ds(pl.multiple_of((g * group + i) * block, block), block), :] = total.astype(BF16)
        dp = dp.astype(BF16)
        dpe[here, :] = dp
        dmix[here, :] = mm_nt(dp, wei[2 * latent :, :]).astype(BF16)
        return 0

    half = (blocks // group) // 2
    lax.fori_loop(0, half, backward, 0)
    if scatter:
        moves[0].step1()
    lax.fori_loop(half, blocks // group, backward, 0)

    put(1, 0, mm_tn(hid[...], dye[...]))
    late = moves[2:]
    if scatter:
        moves[1].start()
        moves[0].step2()
    put(0, 0, mm_tn(edge[...], dpe[...]))
    put(0, latent, mm_tn(flat, dsum[...]))
    put(0, 2 * latent, mm_tn(mixed[...], dpe[...]))
    for move in late:
        move.start()
    if scatter:
        moves[1].step1()

    returns = mm(spread[rows:, :], dmix[...]).astype(BF16)
    for j in range(6):
        rct[j] = returns[j * block : (j + 1) * block]
    behind = Halo(rct, ret, halo_sems, 6, sizes)
    behind.start()
    behind.zero()

    for move in late:
        move.step1()
    if scatter:
        moves[0].step3()
    node_grad[...] += mm(spread[:rows, :], dmix[...]) + mm_nt(
        dsum[...], wei[latent : 2 * latent, :]
    )
    if scatter:
        moves[1].step2()
        for move in late:
            move.step2()
        give_piece(0, moves[0].step4())
        moves[1].step3()

    behind.arrive()
    for n in range(blocks):
        total = node_grad[n * block : (n + 1) * block, :]
        for j in range(6):
            pick = jnp.where(sb[0, j] == n, 1.0, 0.0).astype(F32)
            total = total + ret[j].astype(F32) * pick
        node_grad[n * block : (n + 1) * block, :] = total

    for move in late:
        move.step3()
    if scatter:
        give_piece(1, moves[1].step4())
    for i, move in enumerate(late):
        give_piece(2 + i, move.step4())
    for move in moves:
        move.sent()
    ahead.sent()
    behind.sent()
    edge_done.wait()
    node_done.wait()


def hand_over(*refs):
    count = (len(refs) - 1) // 2
    copies = [
        pltpu.make_async_copy(refs[i], refs[count + i], refs[-1].at[i]) for i in range(count)
    ]
    for copy in copies:
        copy.start()
    for copy in copies:
        copy.wait()


def layer(sizes, *args):
    (node, edge, adj, nb, live, sb, wei, weo, wni, wno, nct, ect) = args
    rows, latent = node.shape
    blocks, degree = nb.shape
    block = adj.shape[-1]
    edges = edge.shape[0]
    devices = sizes["segment"] * sizes["gx"] * sizes["gy"]
    weights = (wei, weo, wni, wno)
    scatter = (
        sizes["segment"] == 2
        and sizes["gx"] == 2
        and sizes["gy"] % CORES == 0
        and all(w.shape[0] % (devices * TILE) == 0 for w in weights)
    )
    shapes = [
        jax.ShapeDtypeStruct((rows, latent), BF16),
        jax.ShapeDtypeStruct((edges, latent), BF16),
        jax.ShapeDtypeStruct((rows, latent), F32),
    ]
    operands = (
        node.reshape(blocks, block, latent),
        edge,
        wei,
        adj.reshape(blocks * degree, block, block),
        weo,
        wni,
        wno,
        nct,
        ect,
    )
    scratch = [pltpu.VMEM(a.shape, a.dtype) for a in operands]
    scratch += [
        pltpu.VMEM((rows, latent), BF16),
        pltpu.VMEM((edges, latent), BF16),
        pltpu.VMEM((6, block, latent), BF16),
        pltpu.VMEM((blocks + 6, block, latent), BF16),
        pltpu.VMEM((6, block, latent), BF16),
        pltpu.VMEM((6, block, latent), BF16),
        pltpu.VMEM((edges, latent), F32),
        pltpu.VMEM(((blocks + 6) * block, edges), BF16),
        pltpu.VMEM((edges, latent), BF16),
        pltpu.VMEM((edges, latent), BF16),
        pltpu.VMEM((edges, latent), F32),
        pltpu.VMEM((edges, latent), F32),
        pltpu.VMEM((edges, 128), F32),
        pltpu.VMEM((rows, latent), BF16),
        pltpu.VMEM((rows, latent), BF16),
        pltpu.VMEM((rows, latent), BF16),
        pltpu.VMEM((rows, latent), BF16),
        pltpu.VMEM((rows, latent), F32),
        pltpu.VMEM((edges, latent), BF16),
        pltpu.VMEM((rows, latent), BF16),
        pltpu.VMEM((edges, latent), BF16),
        pltpu.VMEM((edges, latent), BF16),
        pltpu.SemaphoreType.DMA((11,)),
        pltpu.SemaphoreType.DMA((2, 12)),
    ]
    plan = None
    if scatter:
        own = [w.shape[0] // devices for w in weights]
        shapes += [jax.ShapeDtypeStruct((r * latent // 128, 128), F32) for r in own]
        pieces = {}
        for sub in range(own[2] // TILE):
            pieces[2, sub] = (0, sub * TILE)
        for sub in range(own[3] // TILE):
            pieces[3, sub] = (0, own[2] + sub * TILE)
        for sub in range(own[1] // TILE):
            pieces[1, sub] = (1, sub * TILE)
        for sub in range(own[0] // TILE):
            pieces[0, sub] = (2 + sub, 0)
        heights = [own[2] + own[3], own[1]] + [TILE] * (own[0] // TILE)
        plan = (pieces, own, len(heights))
        s, x, z = sizes["segment"], sizes["gx"], sizes["gy"] // CORES
        scratch += [pltpu.VMEM((s, x, z, CORES, r, latent), BF16) for r in heights]
        for r in heights:
            scratch += [
                pltpu.VMEM((s, x, z, r, latent), BF16),
                pltpu.VMEM((2, z, r, latent), BF16),
                pltpu.VMEM((z, r, latent), BF16),
                pltpu.VMEM((z - 1, r, latent), BF16),
            ]
        scratch.append(pltpu.SemaphoreType.DMA((2, len(heights), 2 + z)))
    else:
        shapes += [jax.ShapeDtypeStruct(w.shape, BF16) for w in weights]
    vmem = pl.BlockSpec(memory_space=pltpu.VMEM)
    smem = pl.BlockSpec(memory_space=pltpu.SMEM)
    hbm = pl.BlockSpec(memory_space=pl.ANY)
    results = pl.pallas_call(
        functools.partial(layer_kernel, sizes, plan, scatter),
        out_shape=shapes,
        in_specs=[smem] * 3 + [hbm] * len(operands),
        out_specs=[hbm, hbm] + [vmem] * 5,
        scratch_shapes=scratch,
        compiler_params=pltpu.CompilerParams(
            collective_id=0, has_side_effects=True, vmem_limit_bytes=60 * 1024 * 1024
        ),
    )(nb.T, live.T, sb, *operands)
    if scatter:
        results = pl.pallas_call(
            hand_over,
            out_shape=shapes,
            in_specs=[hbm] * 7,
            out_specs=[hbm] * 7,
            scratch_shapes=[pltpu.SemaphoreType.DMA((7,))],
            compiler_params=pltpu.CompilerParams(vmem_limit_bytes=60 * 1024 * 1024),
        )(*results)
        shares = [g.reshape(-1) for g in results[3:]]
    else:
        shares = [
            lax.psum_scatter(g.astype(F32).reshape(-1), AXES, scatter_dimension=0, tiled=True)
            for g in results[3:]
        ]
    return tuple(results[:3]) + tuple(shares)


def solution(mesh):
    split, copied = P(AXES, None), P()
    return jax.shard_map(
        functools.partial(layer, dict(mesh.shape)),
        mesh=mesh,
        in_specs=(split, split, P(AXES, None, None, None), split, split, split)
        + (copied,) * 4
        + (split, split),
        out_specs=(split, split, split) + (P(AXES),) * 4,
        check_vma=False,
    )
```

```python
import functools

import jax
import jax.numpy as jnp
from jax import lax
from jax.experimental import pallas as pl
from jax.experimental.pallas import tpu as pltpu
from jax.sharding import PartitionSpec as P

AXES = ("segment", "gx", "gy")
FACES = ("gx", "gy", "segment")
MESH = pl.DeviceIdType.MESH
F32 = jnp.float32
BF16 = jnp.bfloat16
CORES = 2
TILE = 16


def mm(a, b):
    return lax.dot_general(a, b, (((1,), (0,)), ((), ())), preferred_element_type=F32)


def mm_nt(a, b):
    return lax.dot_general(a, b, (((1,), (1,)), ((), ())), preferred_element_type=F32)


def mm_tn(a, b):
    return lax.dot_general(a, b, (((0,), (0,)), ((), ())), preferred_element_type=F32)


def normalised(values):
    centred = values - jnp.mean(values, axis=-1, keepdims=True)
    scale = lax.rsqrt(jnp.mean(centred * centred, axis=-1, keepdims=True) + 1e-05)
    return centred * scale, scale


def normalised_ct(ct, unit, scale):
    return scale * (
        ct
        - jnp.mean(ct, axis=-1, keepdims=True)
        - unit * jnp.mean(ct * unit, axis=-1, keepdims=True)
    )


def silu_and_slope(v):
    gate = 0.5 * jnp.tanh(0.5 * v) + 0.5
    value = v * gate
    return value, gate + value * (1.0 - gate)


class Halo:
    def __init__(self, source, target, sems, first, sizes):
        self.links = []
        for a, axis in enumerate(FACES):
            here = lax.axis_index(axis)
            for step, out, into in ((1, 2 * a + 1, 2 * a), (-1, 2 * a, 2 * a + 1)):
                other = here + step
                to = (other >= 0) & (other < sizes[axis])
                back = here - step
                frm = (back >= 0) & (back < sizes[axis])
                copy = pltpu.make_async_remote_copy(
                    src_ref=source.at[out],
                    dst_ref=target.at[into],
                    send_sem=sems.at[0, first + into],
                    recv_sem=sems.at[1, first + into],
                    device_id={axis: other},
                    device_id_type=MESH,
                )
                self.links.append((to, frm, copy, into))
        self.target = target

    def start(self):
        for to, frm, copy, into in self.links:
            pl.when(to)(copy.start)

    def zero(self):
        for to, frm, copy, into in self.links:

            @pl.when(jnp.logical_not(frm))
            def _(into=into):
                self.target[into] = jnp.zeros(self.target.shape[1:], self.target.dtype)

    def arrive(self):
        for to, frm, copy, into in self.links:
            pl.when(frm)(copy.wait_recv)

    def sent(self):
        for to, frm, copy, into in self.links:
            pl.when(to)(copy.wait_send)


class Scatter:
    def __init__(self, full, r1, r2, r3, rz, sems, piece, sizes):
        self.full, self.r1, self.r2, self.r3, self.rz = full, r1, r2, r3, rz
        self.depth = sizes["gy"] // CORES
        self.seg, self.gx = lax.axis_index("segment"), lax.axis_index("gx")
        gy = lax.axis_index("gy")
        self.core, self.z = lax.rem(gy, CORES), lax.div(gy, CORES)
        self.sem = lambda side, k: sems.at[side, piece, k]

    def copy(self, src, dst, k, to):
        return pltpu.make_async_remote_copy(
            src_ref=src,
            dst_ref=dst,
            send_sem=self.sem(0, k),
            recv_sem=self.sem(1, k),
            device_id=to,
            device_id_type=MESH,
        )

    def core_copy(self):
        other = 1 - self.core
        return self.copy(
            self.full.at[:, :, :, other], self.r1, 0, {"gy": self.z * CORES + other}
        )

    def first_copy(self, core):
        if core == 0:
            return self.copy(self.r1.at[:, 1 - self.gx], self.r2, 1, {"gx": 1 - self.gx})
        return self.copy(self.r1.at[1 - self.seg], self.r2, 1, {"segment": 1 - self.seg})

    def second_copy(self, core):
        if core == 0:
            return self.copy(self.r2.at[1 - self.seg], self.r3, 2, {"segment": 1 - self.seg})
        return self.copy(self.r2.at[1 - self.gx], self.r3, 2, {"gx": 1 - self.gx})

    def last_copy(self, step):
        to = lax.rem(self.z + step, self.depth)
        return self.copy(
            self.r3.at[to], self.rz.at[step - 1], 2 + step, {"gy": to * CORES + self.core}
        )

    def by_core(self, act):
        for core in range(CORES):
            pl.when(self.core == core)(functools.partial(act, core))

    def start(self):
        self.core_copy().start()

    def step1(self):
        self.core_copy().wait_recv()
        for s in range(2):
            for x in range(2):
                for z in range(self.depth):
                    self.r1[s, x, z] = self.r1[s, x, z] + self.full[s, x, z, self.core]
        self.by_core(lambda core: self.first_copy(core).start())

    def step2(self):
        def act(core):
            self.first_copy(core).wait_recv()

            for z in range(self.depth):
                for h in range(2):
                    mine = self.r1[h, self.gx, z] if core == 0 else self.r1[self.seg, h, z]
                    self.r2[h, z] = self.r2[h, z] + mine
            self.second_copy(core).start()

        self.by_core(act)

    def step3(self):
        def act(core):
            self.second_copy(core).wait_recv()
            mine = self.seg if core == 0 else self.gx

            for z in range(self.depth):
                self.r3[z] = self.r3[z] + self.r2[mine, z]

        self.by_core(act)
        for step in range(1, self.depth):
            self.last_copy(step).start()

    def step4(self):
        total = self.r3[self.z].astype(F32)
        for step in range(1, self.depth):
            self.last_copy(step).wait_recv()
            total = total + self.rz[step - 1].astype(F32)
        return total

    def sent(self):
        self.core_copy().wait_send()
        self.by_core(lambda core: self.first_copy(core).wait_send())
        self.by_core(lambda core: self.second_copy(core).wait_send())
        for step in range(1, self.depth):
            self.last_copy(step).wait_send()


def layer_kernel(sizes, plan, scatter, *refs):
    nb, live, sb = refs[:3]
    operands = refs[3:12]
    node_out_hbm, edge_out_hbm, node_grad = refs[12:15]
    grads = refs[15:19]
    held = refs[19:28]
    (node, edge, wei, adj, weo, wni, wno, nct, ect) = held
    (node_out, edge_out, out, ext, rct, ret, pre, spread, mixed, hid, slope, unit, scale, gath, hidn,
     dpren, dyn, dgath, dmix, dsum, dye, dpe, load_sems, halo_sems) = refs[28:52]
    rest = refs[52:]
    blocks, block, latent = node.shape
    degree = adj.shape[0] // blocks
    span = degree * block
    rows = blocks * block

    loads = {}
    for i, (src, dst) in enumerate(zip(operands, held)):
        loads[i] = pltpu.make_async_copy(src, dst, load_sems.at[i])
        loads[i].start()

    gy = lax.axis_index("gy")
    barrier = pltpu.get_barrier_semaphore()
    count = 0
    greet = []
    for axis in FACES:
        here = lax.axis_index(axis)
        for step in (1, -1):
            other = here + step
            there = (other >= 0) & (other < sizes[axis])
            greet.append((there, {axis: other}))
            count = count + there.astype(jnp.int32)
    for there, to in greet:

        @pl.when(there)
        def _(to=to):
            pl.semaphore_signal(barrier, inc=1, device_id=to, device_id_type=MESH)

    if scatter:
        core, z, depth = lax.rem(gy, CORES), lax.div(gy, CORES), sizes["gy"] // CORES
        for step in range(1, depth):
            to = {"gy": lax.rem(z + step, depth) * CORES + core}
            pl.semaphore_signal(barrier, inc=1, device_id=to, device_id_type=MESH)
        count = count + (depth - 1)
    loads[0].wait()
    for j in range(6):
        out[j] = node[sb[0, j]]
    pl.semaphore_wait(barrier, count)

    ahead = Halo(out, ext.at[pl.ds(blocks, 6)], halo_sems, 0, sizes)
    ahead.start()
    ahead.zero()

    moves = []
    if scatter:
        pieces, starts, total = plan
        fulls, bufs, sems = rest[:total], rest[total : 5 * total], rest[5 * total]
        moves = [
            Scatter(fulls[i], *bufs[4 * i : 4 * i + 4], sems, i, sizes) for i in range(total)
        ]

    def put(weight, row, value):
        value = value.astype(BF16)
        if not scatter:
            grads[weight][row : row + value.shape[0], :] = value
            return
        own = starts[weight]
        depth = sizes["gy"] // CORES
        for t in range(0, value.shape[0], TILE):
            d, at = divmod(row + t, own)
            d, c = divmod(d, CORES)
            d, z = divmod(d, depth)
            s, x = divmod(d, sizes["gx"])
            index, base = pieces[weight, at // TILE]
            fulls[index][s, x, z, c, base : base + TILE, :] = value[t : t + TILE]

    def give_piece(index, value):
        for (weight, sub), (piece, base) in pieces.items():
            if piece == index:
                ratio = latent // 128
                for q in range(ratio):
                    part = value[base : base + TILE, q * 128 : (q + 1) * 128]
                    at = sub * TILE * ratio + q
                    grads[weight][pl.ds(at, TILE, stride=ratio), :] = part

    group = 2 if blocks % 2 == 0 else 1
    tall = group * block
    wide = group * span

    loads[1].wait()
    loads[2].wait()
    for n in range(blocks):
        ext[n] = node[n]

    def first(g, _):
        at = pl.multiple_of(g * wide, wide)
        latents = jnp.concatenate([node[g * group + i] for i in range(group)], axis=0)
        own = mm(latents, wei[latent : 2 * latent, :])
        whole = mm(edge[pl.ds(at, wide), :], wei[:latent, :])
        for i in range(group):
            for k in range(degree):
                off = i * span + k * block
                pre[pl.ds(pl.multiple_of(at + off, block), block), :] = (
                    whole[off : off + block] + own[i * block : (i + 1) * block]
                )
        return 0

    lax.fori_loop(0, blocks // group, first, 0)
    loads[3].wait()

    def picked(n, _):
        for k in range(degree):
            turned = adj[n * degree + k].T.astype(F32)
            col = pl.ds(pl.multiple_of(n * span + k * block, block), block)
            for j in range(blocks + 6):
                pick = jnp.where(nb[k, n] == j, 1.0, 0.0).astype(F32)
                spread[j * block : (j + 1) * block, col] = (turned * pick).astype(BF16)
        return 0

    lax.fori_loop(0, blocks, picked, 0)
    loads[4].wait()
    ahead.arrive()

    def forward(g, _):
        at = pl.multiple_of(g * wide, wide)
        here = pl.ds(at, wide)
        for i in range(group):
            n = g * group + i
            for k in range(degree):
                off = pl.multiple_of(at + i * span + k * block, block)
                mixed[pl.ds(off, block), :] = mm(adj[n * degree + k], ext[nb[k, n]]).astype(BF16)
        value, bend = silu_and_slope(pre[here, :] + mm(mixed[here, :], wei[2 * latent :, :]))
        value = value.astype(BF16)
        hid[here, :] = value
        slope[here, :] = bend
        message, spreadness = normalised(mm(value, weo[...]))
        unit[here, :] = message
        scale[here, :] = jnp.broadcast_to(spreadness, (wide, scale.shape[1]))
        edge_out[here, :] = (edge[here, :].astype(F32) + message).astype(BF16)
        for i in range(group):
            n = g * group + i
            off = i * span
            total = message[off : off + block] * live[0, n].astype(F32)
            for k in range(1, degree):
                part = message[off + k * block : off + (k + 1) * block]
                total = total + part * live[k, n].astype(F32)
            gath[pl.ds(pl.multiple_of(n * block, block), block), :] = total.astype(BF16)
        return 0

    lax.fori_loop(0, blocks // group, forward, 0)
    edge_done = pltpu.make_async_copy(edge_out, edge_out_hbm, load_sems.at[9])
    edge_done.start()
    for i in (5, 6, 7):
        loads[i].wait()

    def nodes(g, _):
        at = pl.multiple_of(g * tall, tall)
        here = pl.ds(at, tall)
        latents = jnp.concatenate([node[g * group + i] for i in range(group)], axis=0)
        value, bend = silu_and_slope(
            mm(latents, wni[:latent, :]) + mm(gath[here, :], wni[latent:, :])
        )
        value = value.astype(BF16)
        hidn[here, :] = value
        update, spreadness = normalised(mm(value, wno[...]))
        node_out[here, :] = (latents.astype(F32) + update).astype(BF16)
        ct = nct[here, :].astype(F32)
        dy = normalised_ct(ct, update, spreadness).astype(BF16)
        dyn[here, :] = dy
        dp = (mm_nt(dy, wno[...]) * bend).astype(BF16)
        dpren[here, :] = dp
        node_grad[here, :] = ct + mm_nt(dp, wni[:latent, :])
        dgath[here, :] = mm_nt(dp, wni[latent:, :])
        return 0

    lax.fori_loop(0, blocks // group, nodes, 0)
    node_done = pltpu.make_async_copy(node_out, node_out_hbm, load_sems.at[10])
    node_done.start()

    flat = ext.at[pl.ds(0, blocks)][...].reshape(rows, latent)
    put(2, 0, mm_tn(flat, dpren[...]))
    put(2, latent, mm_tn(gath[...], dpren[...]))
    put(3, 0, mm_tn(hidn[...], dyn[...]))
    if scatter:
        moves[0].start()
    loads[8].wait()

    def backward(g, _):
        at = pl.multiple_of(g * wide, wide)
        here = pl.ds(at, wide)
        back = dgath[pl.ds(pl.multiple_of(g * tall, tall), tall), :]
        ct = ect[here, :].astype(F32) + jnp.concatenate(
            [
                back[i * block : (i + 1) * block] * live[k, g * group + i].astype(F32)
                for i in range(group)
                for k in range(degree)
            ],
            axis=0,
        )
        dy = normalised_ct(ct, unit[here, :], scale[here, :1]).astype(BF16)
        dye[here, :] = dy
        dp = mm_nt(dy, weo[...]) * slope[here, :]
        for i in range(group):
            off = i * span
            total = dp[off : off + block]
            for k in range(1, degree):
                total = total + dp[off + k * block : off + (k + 1) * block]
            dsum[pl.ds(pl.multiple_of((g * group + i) * block, block), block), :] = total.astype(BF16)
        dp = dp.astype(BF16)
        dpe[here, :] = dp
        dmix[here, :] = mm_nt(dp, wei[2 * latent :, :]).astype(BF16)
        return 0

    half = (blocks // group) // 2
    lax.fori_loop(0, half, backward, 0)
    if scatter:
        moves[0].step1()
    lax.fori_loop(half, blocks // group, backward, 0)

    returns = mm(spread[rows:, :], dmix[...]).astype(BF16)
    for j in range(6):
        rct[j] = returns[j * block : (j + 1) * block]
    behind = Halo(rct, ret, halo_sems, 6, sizes)
    behind.start()
    behind.zero()

    put(1, 0, mm_tn(hid[...], dye[...]))
    late = moves[2:]
    if scatter:
        moves[1].start()
        moves[0].step2()
    put(0, 0, mm_tn(edge[...], dpe[...]))
    put(0, latent, mm_tn(flat, dsum[...]))
    put(0, 2 * latent, mm_tn(mixed[...], dpe[...]))
    for move in late:
        move.start()
    if scatter:
        moves[1].step1()

    for move in late:
        move.step1()
    if scatter:
        moves[0].step3()
    node_grad[...] += mm(spread[:rows, :], dmix[...]) + mm_nt(
        dsum[...], wei[latent : 2 * latent, :]
    )
    if scatter:
        moves[1].step2()
        for move in late:
            move.step2()
        give_piece(0, moves[0].step4())
        moves[1].step3()

    behind.arrive()
    for n in range(blocks):
        total = node_grad[n * block : (n + 1) * block, :]
        for j in range(6):
            pick = jnp.where(sb[0, j] == n, 1.0, 0.0).astype(F32)
            total = total + ret[j].astype(F32) * pick
        node_grad[n * block : (n + 1) * block, :] = total

    for move in late:
        move.step3()
    if scatter:
        give_piece(1, moves[1].step4())
    for i, move in enumerate(late):
        give_piece(2 + i, move.step4())
    for move in moves:
        move.sent()
    ahead.sent()
    behind.sent()
    edge_done.wait()
    node_done.wait()


def hand_over(*refs):
    count = (len(refs) - 1) // 3
    first, last, held, sems = refs[:count], refs[count : 2 * count], refs[2 * count : -1], refs[-1]
    into = [pltpu.make_async_copy(first[i], held[i], sems.at[0, i]) for i in range(count)]
    onto = [pltpu.make_async_copy(held[i], last[i], sems.at[1, i]) for i in range(count)]
    for copy in into:
        copy.start()
    for a, b in zip(into, onto):
        a.wait()
        b.start()
    for copy in onto:
        copy.wait()


def layer(sizes, *args):
    (node, edge, adj, nb, live, sb, wei, weo, wni, wno, nct, ect) = args
    rows, latent = node.shape
    blocks, degree = nb.shape
    block = adj.shape[-1]
    edges = edge.shape[0]
    devices = sizes["segment"] * sizes["gx"] * sizes["gy"]
    weights = (wei, weo, wni, wno)
    scatter = (
        sizes["segment"] == 2
        and sizes["gx"] == 2
        and sizes["gy"] % CORES == 0
        and all(w.shape[0] % (devices * TILE) == 0 for w in weights)
    )
    shapes = [
        jax.ShapeDtypeStruct((rows, latent), BF16),
        jax.ShapeDtypeStruct((edges, latent), BF16),
        jax.ShapeDtypeStruct((rows, latent), F32),
    ]
    operands = (
        node.reshape(blocks, block, latent),
        edge,
        wei,
        adj.reshape(blocks * degree, block, block),
        weo,
        wni,
        wno,
        nct,
        ect,
    )
    scratch = [pltpu.VMEM(a.shape, a.dtype) for a in operands]
    scratch += [
        pltpu.VMEM((rows, latent), BF16),
        pltpu.VMEM((edges, latent), BF16),
        pltpu.VMEM((6, block, latent), BF16),
        pltpu.VMEM((blocks + 6, block, latent), BF16),
        pltpu.VMEM((6, block, latent), BF16),
        pltpu.VMEM((6, block, latent), BF16),
        pltpu.VMEM((edges, latent), F32),
        pltpu.VMEM(((blocks + 6) * block, edges), BF16),
        pltpu.VMEM((edges, latent), BF16),
        pltpu.VMEM((edges, latent), BF16),
        pltpu.VMEM((edges, latent), F32),
        pltpu.VMEM((edges, latent), F32),
        pltpu.VMEM((edges, 128), F32),
        pltpu.VMEM((rows, latent), BF16),
        pltpu.VMEM((rows, latent), BF16),
        pltpu.VMEM((rows, latent), BF16),
        pltpu.VMEM((rows, latent), BF16),
        pltpu.VMEM((rows, latent), F32),
        pltpu.VMEM((edges, latent), BF16),
        pltpu.VMEM((rows, latent), BF16),
        pltpu.VMEM((edges, latent), BF16),
        pltpu.VMEM((edges, latent), BF16),
        pltpu.SemaphoreType.DMA((11,)),
        pltpu.SemaphoreType.DMA((2, 12)),
    ]
    plan = None
    if scatter:
        own = [w.shape[0] // devices for w in weights]
        shapes += [jax.ShapeDtypeStruct((r * latent // 128, 128), F32) for r in own]
        pieces = {}
        for sub in range(own[2] // TILE):
            pieces[2, sub] = (0, sub * TILE)
        for sub in range(own[3] // TILE):
            pieces[3, sub] = (0, own[2] + sub * TILE)
        for sub in range(own[1] // TILE):
            pieces[1, sub] = (1, sub * TILE)
        for sub in range(own[0] // TILE):
            pieces[0, sub] = (2 + sub, 0)
        heights = [own[2] + own[3], own[1]] + [TILE] * (own[0] // TILE)
        plan = (pieces, own, len(heights))
        s, x, z = sizes["segment"], sizes["gx"], sizes["gy"] // CORES
        scratch += [pltpu.VMEM((s, x, z, CORES, r, latent), BF16) for r in heights]
        for r in heights:
            scratch += [
                pltpu.VMEM((s, x, z, r, latent), BF16),
                pltpu.VMEM((2, z, r, latent), BF16),
                pltpu.VMEM((z, r, latent), BF16),
                pltpu.VMEM((z - 1, r, latent), BF16),
            ]
        scratch.append(pltpu.SemaphoreType.DMA((2, len(heights), 2 + z)))
    else:
        shapes += [jax.ShapeDtypeStruct(w.shape, BF16) for w in weights]
    vmem = pl.BlockSpec(memory_space=pltpu.VMEM)
    smem = pl.BlockSpec(memory_space=pltpu.SMEM)
    hbm = pl.BlockSpec(memory_space=pl.ANY)
    results = pl.pallas_call(
        functools.partial(layer_kernel, sizes, plan, scatter),
        out_shape=shapes,
        in_specs=[smem] * 3 + [hbm] * len(operands),
        out_specs=[hbm, hbm] + [vmem] * 5,
        scratch_shapes=scratch,
        compiler_params=pltpu.CompilerParams(
            collective_id=0, has_side_effects=True, vmem_limit_bytes=60 * 1024 * 1024
        ),
    )(nb.T, live.T, sb, *operands)
    if scatter:
        results = pl.pallas_call(
            hand_over,
            out_shape=shapes,
            in_specs=[hbm] * 7,
            out_specs=[hbm] * 7,
            scratch_shapes=[pltpu.VMEM(a.shape, a.dtype) for a in shapes]
            + [pltpu.SemaphoreType.DMA((2, 7))],
            compiler_params=pltpu.CompilerParams(vmem_limit_bytes=60 * 1024 * 1024),
        )(*results)
        shares = [g.reshape(-1) for g in results[3:]]
    else:
        shares = [
            lax.psum_scatter(g.astype(F32).reshape(-1), AXES, scatter_dimension=0, tiled=True)
            for g in results[3:]
        ]
    return tuple(results[:3]) + tuple(shares)


def solution(mesh):
    split, copied = P(AXES, None), P()
    return jax.shard_map(
        functools.partial(layer, dict(mesh.shape)),
        mesh=mesh,
        in_specs=(split, split, P(AXES, None, None, None), split, split, split)
        + (copied,) * 4
        + (split, split),
        out_specs=(split, split, split) + (P(AXES),) * 4,
        check_vma=False,
    )
```
